256 devices in a mesh: outer: 16 (over z, y_lo), inner: 16 (over x, y_hi, core).
Axes of the slice: x: 4, y: 4 (y_hi: 2, y_lo: 2; y = y_hi * 2 + y_lo), z: 8, core: 2. Of those that a mesh axis runs over, the one named last changes fastest.
Arguments:
- queries: bfloat16 [131072, 1024], P(('outer', 'inner')), may hold values from -8 to 8
- keys: bfloat16 [131072, 1024], P(('outer', 'inner')), may hold values from -8 to 8
- values: bfloat16 [131072, 1024], P(('outer', 'inner')), may hold values from -6 to 6
- offsets: int32 [4, 8], replicated, may hold values from 0 to 7, as said below
Outputs:
- mixed: bfloat16 [131072, 1024], P(('outer', 'inner'))
The draws below stay inside these ranges and needn't reach their ends.
Inputs may be any that keep to these rules, and one draw needn't show every extreme that they name: offsets[b, h] lies in 0 to 2^b - 1.
All inputs are finite; a program needn't handle non-finite values.
Results may differ from the reference program's by a relative error of at most 0.0032.
Values may be sent and summed in bfloat16 or wider, within the bound.
A program may use at most 192 MiB of HBM per device.

```python
import jax
import jax.numpy as jnp
from jax import lax

H = 8
DH = 128
KEYS = 2048
BRANCHES = 4
SEQ = 131072


def draw_queries(key, part):
    key = jax.random.fold_in(key, 1)
    result = 2.0 * jax.random.normal(key, (SEQ, H * DH))
    return jnp.clip(result, -8.0, 8.0).astype(jnp.bfloat16)


def draw_keys(key, part):
    key = jax.random.fold_in(key, 2)
    result = jax.random.normal(key, (SEQ, H * DH))
    return jnp.clip(result, -8.0, 8.0).astype(jnp.bfloat16)


def draw_offsets(key, part):
    key = jax.random.fold_in(key, 3)
    limits = 2 ** jnp.arange(BRANCHES, dtype=jnp.int32)
    base_draw = jax.random.randint(key, (BRANCHES, H), 0, limits[:, None]).astype(jnp.int32)
    top_head = jax.random.randint(jax.random.fold_in(key, 9), (BRANCHES,), 0, H).astype(jnp.int32)
    at_top = jnp.arange(H, dtype=jnp.int32)[None, :] == top_head[:, None]
    return jnp.where(at_top, (limits - 1)[:, None], base_draw).astype(jnp.int32)


def level_of(own_key, dims, shards, low, high):
    loudness = 1.0
    for axis_at, shards_of in shards:
        steps = jax.random.uniform(jax.random.fold_in(jax.random.fold_in(own_key, 6), axis_at), (shards_of,), jnp.float32, low / len(shards), high / len(shards))
        loudness = loudness * jnp.repeat(jnp.exp(steps), dims[axis_at] // shards_of).reshape((-1,) + (1,) * (len(dims) - 1 - axis_at))
    return loudness


def bell_draw(own_key, shape, deviation, reach, cuts=(), held_as=jnp.bfloat16):
    loudness = level_of(own_key, shape, cuts, -0.22, 0.18) if cuts else 1.0
    entries = jax.random.normal(own_key, shape, jnp.float32) * deviation * loudness
    return jnp.minimum(jnp.maximum(entries, -reach), reach).astype(held_as)


def setup_inputs(seed: int = 0) -> dict:
    arg_keys = jax.random.split(jax.random.key(seed), 5)
    queries = draw_queries(jax.random.fold_in(arg_keys[4], 71), 0)
    keys = draw_keys(jax.random.fold_in(arg_keys[4], 71), 0)
    values = bell_draw(arg_keys[2], (SEQ, H * DH), 1.0, 6.0, ((0, 256),))
    offsets = draw_offsets(jax.random.fold_in(arg_keys[4], 71), 0)
    return {"queries": queries, "keys": keys, "values": values, "offsets": offsets}


negative_fill = -1e30


def select_rows(matrix, offsets_row, dilation, head_count):
    head_dim = matrix.shape[1] // head_count
    blocks = matrix.reshape(matrix.shape[0] // dilation, dilation, head_count, head_dim)
    picker = jnp.arange(dilation, dtype=jnp.int32)[:, None] == offsets_row[None, :].astype(jnp.int32)
    picked = jnp.einsum("jrhd,rh->hjd", blocks.astype(jnp.float32), picker.astype(jnp.float32))
    return picked.astype(jnp.bfloat16), picker


def attend(queries_sel, keys_sel, values_sel, query_start):
    head_dim = queries_sel.shape[-1]
    scores = jnp.einsum("hsqd,hskd->hsqk", queries_sel.astype(jnp.float32), keys_sel.astype(jnp.float32))
    scores = scores * (head_dim ** -0.5)
    query_pos = query_start + jnp.arange(queries_sel.shape[2], dtype=jnp.int32)
    key_pos = jnp.arange(keys_sel.shape[2], dtype=jnp.int32)
    allowed = key_pos[None, :] <= query_pos[:, None]
    scores = jnp.where(allowed, scores, negative_fill)
    row_max = jnp.max(scores, axis=-1)
    weights = jnp.where(allowed, jnp.exp(scores - row_max[..., None]), 0.0)
    row_sum = jnp.sum(weights, axis=-1)
    rounded = lax.optimization_barrier(weights.astype(jnp.bfloat16)).astype(jnp.float32)
    weighted = jnp.einsum("hsqk,hskd->hsqd", rounded, values_sel.astype(jnp.float32))
    return row_max, row_sum, weighted


def spread(row_max, row_sum, weighted, picker):
    chosen = picker[None]
    head_count = row_max.shape[0]
    head_dim = weighted.shape[-1]
    full_max = jnp.where(chosen, row_max.T[:, None, :], negative_fill).reshape(-1, head_count)
    full_sum = jnp.where(chosen, row_sum.T[:, None, :], 0.0).reshape(-1, head_count)
    full_weighted = jnp.where(chosen[..., None], jnp.transpose(weighted, (1, 0, 2))[:, None], 0.0)
    return full_max, full_sum, full_weighted.reshape(-1, head_count, head_dim)


def combine(earlier, current):
    new_max = jnp.maximum(earlier[0], current[0])
    factor_old = jnp.exp(earlier[0] - new_max)
    factor_new = jnp.exp(current[0] - new_max)
    new_sum = earlier[1] * factor_old + current[1] * factor_new
    new_weighted = earlier[2] * factor_old[..., None] + current[2] * factor_new[..., None]
    return new_max, new_sum, new_weighted


def per_segment(segment_items):
    return attend(segment_items[0], segment_items[1], segment_items[2], 0)


def reference(queries, keys, values, offsets):
    head_count = offsets.shape[1]
    seq_total = queries.shape[0]
    head_dim = queries.shape[1] // head_count
    running = None
    for branch in range(BRANCHES):
        dilation = 2 ** branch
        picked_queries, picker = select_rows(queries, offsets[branch], dilation, head_count)
        picked_keys, picker = select_rows(keys, offsets[branch], dilation, head_count)
        picked_values, picker = select_rows(values, offsets[branch], dilation, head_count)
        row_count = seq_total // dilation
        segments = row_count // KEYS

        def by_segment(picked):
            return picked.reshape(head_count, segments, KEYS, head_dim).transpose(1, 0, 2, 3)[:, :, None]

        row_max, row_sum, weighted = lax.map(per_segment, (by_segment(picked_queries), by_segment(picked_keys), by_segment(picked_values)))
        row_max = row_max.reshape(segments, head_count, KEYS).transpose(1, 0, 2).reshape(head_count, row_count)
        row_sum = row_sum.reshape(segments, head_count, KEYS).transpose(1, 0, 2).reshape(head_count, row_count)
        weighted = weighted.reshape(segments, head_count, KEYS, head_dim).transpose(1, 0, 2, 3).reshape(head_count, row_count, head_dim)
        branch_state = spread(row_max, row_sum, weighted, picker)
        running = branch_state if running is None else combine(running, branch_state)
    result = running[2] / running[1][..., None]
    return result.reshape(seq_total, head_count * head_dim).astype(jnp.bfloat16)
```

```python
import functools
import math

import jax
import jax.numpy as jnp
from jax import lax
from jax.experimental import pallas as pl
from jax.experimental.pallas import tpu as pltpu
from jax.sharding import PartitionSpec as P

KEYS = 2048
BRANCHES = 4
HEADS = 8
DH = 128
ROWS = 512
GROUP = 16
SLOTS = 8
SPAN = SLOTS * ROWS
TILE = 256
MESH = pl.DeviceIdType.MESH

QUERY_BASE = (0, 4096, 6144, 7168)
QUERY_ROWS = 7680
KEY_BASE = (0, 4096, 6144, 8192)
KEY_ROWS = 10240
LOG2E = math.log2(math.e)
TO_LOG2 = LOG2E * DH**-0.5
NEGATIVE = -1e30
STEPS = ((0, 0), (2, 1), (1, 0), (3, 1), (0, 1), (2, 0), (1, 1), (3, 0))


def kernel(
    off_ref, q_hbm, k_hbm, v_hbm, out_hbm,
    qa, ka, va, wide, probs, scores, lse, outs, rep_out, rep_lse, packed,
    in_send, in_recv, half_send, half_recv, far_send, far_recv, out_send, out_recv,
):
    outer, inner = lax.axis_index("outer"), lax.axis_index("inner")
    head, half = inner // 2, inner % 2
    x, y_hi = inner // 4, (inner // 2) % 2
    own_slot, own_half = inner % SLOTS, inner // SLOTS
    y_lo = outer % 2
    quarter = 2 * y_lo + half
    offs = [off_ref[b, head] for b in range(BRANCHES)]

    barrier = pltpu.get_barrier_semaphore()
    for d in range(1, GROUP):
        pl.semaphore_signal(
            barrier, inc=1, device_id=(outer, lax.rem(inner + d, GROUP)), device_id_type=MESH
        )
    other = outer + 1 - 2 * y_lo
    for core in range(2):
        pl.semaphore_signal(
            barrier, inc=1, device_id=(other, 2 * head + core), device_id_type=MESH
        )
    pl.semaphore_wait(barrier, GROUP + 1)

    sources, buffers = (q_hbm, k_hbm, v_hbm), (qa, ka, va)

    def in_copy(a, t):
        dx, dy = STEPS[t]
        to_head = lax.rem(x + dx, 4) * 2 + lax.rem(y_hi + dy, 2)
        src = sources[a].at[:, pl.ds(pl.multiple_of(to_head * DH, DH), DH)]
        dst = buffers[a].at[pl.ds(pl.multiple_of(own_slot * ROWS, ROWS), ROWS)]
        return src, dst, 2 * to_head + own_half

    def in_remote(a, t):
        src, dst, target = in_copy(a, t)
        return pltpu.make_async_remote_copy(
            src_ref=src, dst_ref=dst, send_sem=in_send.at[a, t], recv_sem=in_recv.at[a, own_slot],
            device_id=(outer, target), device_id_type=MESH,
        )

    stays = half == own_half
    for a in range(3):
        @pl.when(stays)
        def _():
            src, dst, _ = in_copy(a, 0)
            pltpu.make_async_copy(src, dst, in_recv.at[a, own_slot]).start()

        @pl.when(jnp.logical_not(stays))
        def _():
            in_remote(a, 0).start()

        for t in range(1, len(STEPS)):
            in_remote(a, t).start()

    def wait_in(a, first, last):
        for slot in range(first, last):
            rows = buffers[a].at[pl.ds(slot * ROWS, ROWS)]
            pltpu.make_async_copy(rows, rows, in_recv.at[a, slot]).wait()

    def select(a):
        buffer = buffers[a]
        bases = QUERY_BASE if a == 0 else KEY_BASE
        shift = (0, 0, 0, 0) if a == 0 else (0, 0, half * (SPAN // 4), quarter * (SPAN // 8))

        @pl.loop(0, SLOTS)
        def _(j):
            rows = pl.ds(pl.multiple_of(j * ROWS, ROWS), ROWS)
            wide[rows, :] = buffer[rows, :].astype(jnp.float32)

        for b in range(1, BRANCHES):
            r = 2**b

            @pl.loop(0, SPAN // r // TILE)
            def _(j):
                picked = wide[pl.ds(offs[b] + j * (TILE * r), TILE, stride=r), :]
                at = pl.multiple_of(bases[b] + shift[b] + j * TILE, TILE)
                buffer[pl.ds(at, TILE), :] = picked.astype(jnp.bfloat16)

    def half_copy(a):
        rows = buffers[a].at[pl.ds(KEY_BASE[2], SPAN // 4)]
        return pltpu.make_async_remote_copy(
            src_ref=rows, dst_ref=rows, send_sem=half_send.at[a - 1], recv_sem=half_recv.at[a - 1],
            device_id=(outer, 2 * head + 1), device_id_type=MESH,
        )

    def far_rows(a, at):
        return buffers[a].at[pl.ds(pl.multiple_of(KEY_BASE[3] + at * ROWS, ROWS), ROWS)]

    def far_copy(a, to):
        return pltpu.make_async_remote_copy(
            src_ref=far_rows(a, quarter), dst_ref=far_rows(a, quarter),
            send_sem=far_send.at[a - 1, to], recv_sem=far_recv.at[a - 1, quarter],
            device_id=(outer - y_lo + to // 2, 2 * head + to % 2), device_id_type=MESH,
        )

    def send_earlier(a):
        @pl.when(half == 0)
        def _():
            half_copy(a).start()

        for to in range(1, 4):
            @pl.when(quarter < to)
            def _():
                far_copy(a, to).start()

    def wait_half(a):
        @pl.when(half == 1)
        def _():
            rows = buffers[a].at[pl.ds(KEY_BASE[2], SPAN // 4)]
            pltpu.make_async_copy(rows, rows, half_recv.at[a - 1]).wait()

    def wait_far(a):
        for source in range(3):
            @pl.when(quarter > source)
            def _():
                rows = far_rows(a, source)
                pltpu.make_async_copy(rows, rows, far_recv.at[a - 1, source]).wait()

    def query_at(segment, count):
        first = jnp.where(segment == 3, 4 * half, jnp.where(segment == 4, 2 * quarter, 0))
        base = jnp.where(segment == 4, QUERY_BASE[3], segment * KEYS)
        return pl.multiple_of(base + (count - 1 - first) * TILE, TILE)

    def when_there(segment, count):
        low = jnp.where(segment == 3, 4 * half, jnp.where(segment == 4, 2 * quarter, 0))
        high = jnp.where(segment == 3, low + 4, jnp.where(segment == 4, low + 2, 8))
        return jnp.logical_and(count > low, count <= high)

    allowed = lax.broadcasted_iota(jnp.int32, (TILE, TILE), 1) <= lax.broadcasted_iota(
        jnp.int32, (TILE, TILE), 0
    )

    def weigh(segment, count):
        rows = pl.ds(query_at(segment, count), TILE)
        queries = qa[rows, :]
        tops = None
        for j in range(count):
            keys = ka[pl.ds(pl.multiple_of(segment * KEYS + j * TILE, TILE), TILE), :]
            s = lax.dot_general(
                queries, keys, (((1,), (1,)), ((), ())), preferred_element_type=jnp.float32
            )
            if j == count - 1:
                s = jnp.where(allowed, s, NEGATIVE)
            scores[:, j * TILE : (j + 1) * TILE] = s
            top = jnp.maximum(s[:, :128], s[:, 128:])
            tops = top if tops is None else jnp.maximum(tops, top)
        top = jnp.max(tops, axis=1, keepdims=True)
        sums = None
        for j in range(count):
            p = jnp.exp2((scores[:, j * TILE : (j + 1) * TILE] - top) * TO_LOG2)
            part = p[:, :128] + p[:, 128:]
            sums = part if sums is None else sums + part
            probs[rows, j * TILE : (j + 1) * TILE] = p.astype(jnp.bfloat16)
        total = jnp.sum(sums, axis=1, keepdims=True)
        lse[rows, :] = jnp.broadcast_to(top * TO_LOG2 + jnp.log(total) * LOG2E, (TILE, DH))
        outs[rows, :] = jnp.broadcast_to(1.0 / total, (TILE, DH))

    def mix(segment, count):
        rows = pl.ds(query_at(segment, count), TILE)
        weighted = jnp.dot(
            probs[rows, : count * TILE],
            va[pl.ds(pl.multiple_of(segment * KEYS, KEYS), count * TILE), :],
            preferred_element_type=jnp.float32,
        )
        outs[rows, :] = weighted * outs[rows, :]

    def each(step, segment):
        for count in range(1, KEYS // TILE + 1):
            @pl.when(when_there(segment, count))
            def _():
                step(segment, count)

    for a in (0, 1):
        wait_in(a, 0, SLOTS)
    select(1)
    send_earlier(1)
    select(0)

    @pl.loop(0, 5)
    def _(segment):
        @pl.when(segment == 3)
        def _():
            wait_half(1)
            wait_far(1)

        each(weigh, segment)

    wait_in(2, 0, SLOTS)
    select(2)
    send_earlier(2)

    @pl.loop(0, 5)
    def _(segment):
        @pl.when(segment == 3)
        def _():
            wait_half(2)
            wait_far(2)

        each(mix, segment)

    def home_copy(j):
        dst = out_hbm.at[:, pl.ds(pl.multiple_of(head * DH, DH), DH)]
        return packed.at[j], dst, SLOTS * half + j

    def home_remote(j):
        src, dst, target = home_copy(j)
        return pltpu.make_async_remote_copy(
            src_ref=src, dst_ref=dst, send_sem=out_send.at[j], recv_sem=out_recv.at[head],
            device_id=(outer, target), device_id_type=MESH,
        )

    @pl.loop(0, SLOTS)
    def _(j):
        for b in range(1, BRANCHES):
            r = 2**b
            count = ROWS // r
            rows = pl.ds(pl.multiple_of(QUERY_BASE[b] + j * count, count), count)
            out_b, lse_b = outs[rows, :], lse[rows, :]
            for at in range(r):
                rep_out[b - 1, pl.ds(at, count, stride=r), :] = out_b
                rep_lse[b - 1, pl.ds(at, count, stride=r), :] = lse_b

        @pl.loop(0, ROWS // 128)
        def _(part):
            at = pl.multiple_of(part * 128, 128)
            here = pl.ds(at, 128)
            row = lax.broadcasted_iota(jnp.int32, (128, DH), 0)
            base = pl.ds(pl.multiple_of(j * ROWS + part * 128, 128), 128)
            levels = [lse[base, :]]
            terms = [outs[base, :]]
            for b in range(1, BRANCHES):
                chosen = lax.bitwise_and(row, 2**b - 1) == offs[b]
                levels.append(jnp.where(chosen, rep_lse[b - 1, here, :], NEGATIVE))
                terms.append(rep_out[b - 1, here, :])
            top = functools.reduce(jnp.maximum, levels)
            weights = [jnp.exp2(level - top) for level in levels]
            above = sum(w * t for w, t in zip(weights, terms))
            packed[j, here, :] = (above / sum(weights)).astype(jnp.bfloat16)

        target = SLOTS * half + j

        @pl.when(target == inner)
        def _():
            src, dst, _ = home_copy(j)
            pltpu.make_async_copy(src, dst, out_recv.at[head]).start()

        @pl.when(target != inner)
        def _():
            home_remote(j).start()

    for a in range(3):
        for t in range(len(STEPS)):
            if t == 0:
                @pl.when(jnp.logical_not(stays))
                def _():
                    in_remote(a, 0).wait_send()
            else:
                in_remote(a, t).wait_send()
    for a in (1, 2):
        @pl.when(half == 0)
        def _():
            half_copy(a).wait_send()

        for to in range(1, 4):
            @pl.when(quarter < to)
            def _():
                far_copy(a, to).wait_send()
    for j in range(SLOTS):
        @pl.when(SLOTS * half + j != inner)
        def _():
            home_remote(j).wait_send()
    for h in range(HEADS):
        columns = out_hbm.at[:, h * DH : (h + 1) * DH]
        pltpu.make_async_copy(columns, columns, out_recv.at[h]).wait()


def local(queries, keys, values, offsets):
    anywhere = pl.BlockSpec(memory_space=pl.ANY)
    return pl.pallas_call(
        kernel,
        out_shape=jax.ShapeDtypeStruct((ROWS, HEADS * DH), jnp.bfloat16),
        in_specs=[pl.BlockSpec(memory_space=pltpu.SMEM), anywhere, anywhere, anywhere],
        out_specs=anywhere,
        scratch_shapes=[
            pltpu.VMEM((QUERY_ROWS, DH), jnp.bfloat16),
            pltpu.VMEM((KEY_ROWS, DH), jnp.bfloat16),
            pltpu.VMEM((KEY_ROWS, DH), jnp.bfloat16),
            pltpu.VMEM((SPAN, DH), jnp.float32),
            pltpu.VMEM((QUERY_ROWS, KEYS), jnp.bfloat16),
            pltpu.VMEM((TILE, KEYS), jnp.float32),
            pltpu.VMEM((QUERY_ROWS, DH), jnp.float32),
            pltpu.VMEM((QUERY_ROWS, DH), jnp.float32),
            pltpu.VMEM((BRANCHES - 1, ROWS, DH), jnp.float32),
            pltpu.VMEM((BRANCHES - 1, ROWS, DH), jnp.float32),
            pltpu.VMEM((SLOTS, ROWS, DH), jnp.bfloat16),
            pltpu.SemaphoreType.DMA((3, SLOTS)),
            pltpu.SemaphoreType.DMA((3, SLOTS)),
            pltpu.SemaphoreType.DMA((2,)),
            pltpu.SemaphoreType.DMA((2,)),
            pltpu.SemaphoreType.DMA((2, 4)),
            pltpu.SemaphoreType.DMA((2, 4)),
            pltpu.SemaphoreType.DMA((SLOTS,)),
            pltpu.SemaphoreType.DMA((HEADS,)),
        ],
        compiler_params=pltpu.CompilerParams(
            collective_id=0, has_side_effects=True, vmem_limit_bytes=60 * 2**20
        ),
        name="attention",
    )(offsets, queries, keys, values)


def solution(mesh):
    return jax.shard_map(
        local,
        mesh=mesh,
        in_specs=(
            P(("outer", "inner"), None),
            P(("outer", "inner"), None),
            P(("outer", "inner"), None),
            P(),
        ),
        out_specs=P(("outer", "inner"), None),
        check_vma=False,
    )
```

```python
import functools
import math

import jax
import jax.numpy as jnp
from jax import lax
from jax.experimental import pallas as pl
from jax.experimental.pallas import tpu as pltpu
from jax.sharding import PartitionSpec as P

KEYS = 2048
BRANCHES = 4
HEADS = 8
DH = 128
ROWS = 512
GROUP = 16
SLOTS = 8
SPAN = SLOTS * ROWS
PICKED = ROWS // 8
TILE = 256
MESH = pl.DeviceIdType.MESH

QUERY_BASE = (0, 4096, 6144, 7168)
QUERY_ROWS = 7680
KEY_BASE = (0, 4096, 6144, 8192)
KEY_ROWS = 10240
LOG2E = math.log2(math.e)
TO_LOG2 = LOG2E * DH**-0.5
NEGATIVE = -1e30
STEPS = ((0, 0), (2, 1), (1, 0), (3, 1), (0, 1), (2, 0), (1, 1), (3, 0))


def kernel(
    off_ref, q_hbm, k_hbm, v_hbm, out_hbm,
    qa, ka, va, wide, home, far, probs, scores, lse, outs, rep_out, rep_lse, packed,
    in_send, in_recv, home_sem, far_send, far_recv, side_send, side_recv, out_send, out_recv,
):
    outer, inner = lax.axis_index("outer"), lax.axis_index("inner")
    head, half = inner // 2, inner % 2
    x, y_hi = inner // 4, (inner // 2) % 2
    own_slot, own_half = inner % SLOTS, inner // SLOTS
    y_lo = outer % 2
    quarter = 2 * y_lo + half
    offs = [off_ref[b, head] for b in range(BRANCHES)]

    barrier = pltpu.get_barrier_semaphore()
    for d in range(1, GROUP):
        pl.semaphore_signal(
            barrier, inc=1, device_id=(outer, lax.rem(inner + d, GROUP)), device_id_type=MESH
        )
    @pl.when(y_lo == 0)
    def _():
        for h in range(HEADS):
            pl.semaphore_signal(
                barrier, inc=1, device_id=(outer + 1, 2 * h + own_half), device_id_type=MESH
            )

    @pl.when(y_lo == 1)
    def _():
        for slot in range(SLOTS):
            pl.semaphore_signal(
                barrier, inc=1, device_id=(outer - 1, SLOTS * half + slot), device_id_type=MESH
            )

    @pl.when(y_lo == 0)
    def _():
        for a, source in ((0, k_hbm), (1, v_hbm)):
            load = pltpu.make_async_copy(source, home.at[a], home_sem.at[a])
            load.start()
        for a, source in ((0, k_hbm), (1, v_hbm)):
            pltpu.make_async_copy(source, home.at[a], home_sem.at[a]).wait()
            for h in range(HEADS):
                wide[...] = home[a, :, h * DH : (h + 1) * DH].astype(jnp.float32)
                picked = wide[pl.ds(off_ref[3, h], PICKED, stride=8), :]
                far[a, h * PICKED : (h + 1) * PICKED, :] = picked.astype(jnp.bfloat16)

    pl.semaphore_wait(barrier, GROUP - 1 + SLOTS)

    sources, buffers = (q_hbm, k_hbm, v_hbm), (qa, ka, va)

    def in_copy(a, t):
        dx, dy = STEPS[t]
        to_head = lax.rem(x + dx, 4) * 2 + lax.rem(y_hi + dy, 2)
        src = sources[a].at[:, pl.ds(pl.multiple_of(to_head * DH, DH), DH)]
        dst = buffers[a].at[pl.ds(pl.multiple_of(own_slot * ROWS, ROWS), ROWS)]
        return src, dst, 2 * to_head + own_half

    def in_remote(a, t):
        src, dst, target = in_copy(a, t)
        return pltpu.make_async_remote_copy(
            src_ref=src, dst_ref=dst, send_sem=in_send.at[a, t], recv_sem=in_recv.at[a, own_slot],
            device_id=(outer, target), device_id_type=MESH,
        )

    stays = half == own_half

    def send_in(a):
        @pl.when(stays)
        def _():
            src, dst, _ = in_copy(a, 0)
            pltpu.make_async_copy(src, dst, in_recv.at[a, own_slot]).start()

        @pl.when(jnp.logical_not(stays))
        def _():
            in_remote(a, 0).start()

        for t in range(1, len(STEPS)):
            in_remote(a, t).start()

    def far_copy(a, h):
        rows = buffers[a].at[
            pl.ds(pl.multiple_of(KEY_BASE[3] + own_half * ROWS + own_slot * PICKED, PICKED), PICKED)
        ]
        return pltpu.make_async_remote_copy(
            src_ref=far.at[a - 1, pl.ds(h * PICKED, PICKED)], dst_ref=rows,
            send_sem=far_send.at[a - 1, h], recv_sem=far_recv.at[a - 1, own_slot],
            device_id=(outer + 1, 2 * h + own_half), device_id_type=MESH,
        )

    def send_far(a):
        for h in range(HEADS):
            far_copy(a, h).start()

    send_in(1)
    send_in(0)

    @pl.when(y_lo == 0)
    def _():
        send_far(1)
        send_far(2)

    send_in(2)

    def take(a, slot):
        buffer = buffers[a]
        bases = QUERY_BASE if a == 0 else KEY_BASE
        shift = (0, 0, 0, 0) if a == 0 else (0, 0, half * (SPAN // 4), quarter * (SPAN // 8))
        rows = pl.ds(pl.multiple_of(slot * ROWS, ROWS), ROWS)
        arrived = buffer.at[rows]
        pltpu.make_async_copy(arrived, arrived, in_recv.at[a, slot]).wait()
        wide[...] = buffer[rows, :].astype(jnp.float32)
        for b in range(1, BRANCHES):
            count = ROWS >> b
            picked = wide[pl.ds(offs[b], count, stride=2**b), :]
            at = pl.multiple_of(bases[b] + shift[b] + slot * count, count)
            buffer[pl.ds(at, count), :] = picked.astype(jnp.bfloat16)

    def sibling_copy(a, kind):
        if kind == 0:
            rows = buffers[a].at[pl.ds(KEY_BASE[2], SPAN // 4)]
        elif kind == 1:
            rows = buffers[a].at[pl.ds(pl.multiple_of(KEY_BASE[3] + quarter * ROWS, ROWS), ROWS)]
        else:
            rows = buffers[a].at[pl.ds(pl.multiple_of(KEY_BASE[3] + half * ROWS, ROWS), ROWS)]
        return pltpu.make_async_remote_copy(
            src_ref=rows, dst_ref=rows,
            send_sem=side_send.at[a - 1, kind], recv_sem=side_recv.at[a - 1, kind],
            device_id=(outer, 2 * head + 1 - half), device_id_type=MESH,
        )

    def send_sibling(a):
        @pl.when(half == 0)
        def _():
            for kind in range(2):
                sibling_copy(a, kind).start()

    def swap_far():
        @pl.when(y_lo == 1)
        def _():
            for a in (1, 2):
                for slot in range(SLOTS):
                    rows = buffers[a].at[
                        pl.ds(pl.multiple_of(KEY_BASE[3] + half * ROWS + slot * PICKED, PICKED), PICKED)
                    ]
                    pltpu.make_async_copy(rows, rows, far_recv.at[a - 1, slot]).wait()
                sibling_copy(a, 2).start()

    def wait_rows(a, kind, first, count):
        rows = buffers[a].at[pl.ds(first, count)]
        pltpu.make_async_copy(rows, rows, side_recv.at[a - 1, kind]).wait()

    def wait_sibling(a):
        @pl.when(half == 1)
        def _():
            wait_rows(a, 0, KEY_BASE[2], SPAN // 4)
            wait_rows(a, 1, pl.multiple_of(KEY_BASE[3] + 2 * y_lo * ROWS, ROWS), ROWS)

    def wait_swap(a):
        @pl.when(y_lo == 1)
        def _():
            wait_rows(a, 2, pl.multiple_of(KEY_BASE[3] + (1 - half) * ROWS, ROWS), ROWS)

    allowed = lax.broadcasted_iota(jnp.int32, (TILE, TILE), 1) <= lax.broadcasted_iota(
        jnp.int32, (TILE, TILE), 0
    )

    def tasks(branch, first, last, before=0, segment=0):
        query = QUERY_BASE[branch] + segment * KEYS
        key = KEY_BASE[branch] + segment * KEYS
        return [(query + i * TILE, key, before + i + 1) for i in range(first, last)]

    def weigh(group):
        for n, (query, key, count) in enumerate(group):
            rows = slice(query, query + TILE)
            queries = qa[rows, :]
            tops = None
            for j in range(count):
                keys = ka[key + j * TILE : key + (j + 1) * TILE, :]
                s = lax.dot_general(
                    queries, keys, (((1,), (1,)), ((), ())), preferred_element_type=jnp.float32
                )
                if j == count - 1:
                    s = jnp.where(allowed, s, NEGATIVE)
                scores[n, :, j * TILE : (j + 1) * TILE] = s
                top = jnp.maximum(s[:, :128], s[:, 128:])
                tops = top if tops is None else jnp.maximum(tops, top)
            top = jnp.max(tops, axis=1, keepdims=True)
            sums = None
            for j in range(count):
                p = jnp.exp2((scores[n, :, j * TILE : (j + 1) * TILE] - top) * TO_LOG2)
                part = p[:, :128] + p[:, 128:]
                sums = part if sums is None else sums + part
                probs[rows, j * TILE : (j + 1) * TILE] = p.astype(jnp.bfloat16)
            total = jnp.sum(sums, axis=1, keepdims=True)
            lse[rows, :] = jnp.broadcast_to(top * TO_LOG2 + jnp.log(total) * LOG2E, (TILE, DH))
            outs[rows, :] = jnp.broadcast_to(1.0 / total, (TILE, DH))

    def mix(group):
        for query, key, count in group:
            rows = slice(query, query + TILE)
            weighted = jnp.dot(
                probs[rows, : count * TILE],
                va[key : key + count * TILE, :],
                preferred_element_type=jnp.float32,
            )
            outs[rows, :] = weighted * outs[rows, :]

    @pl.loop(0, SLOTS)
    def _(slot):
        take(1, slot)

    send_sibling(1)

    @pl.loop(0, SLOTS)
    def _(slot):
        take(0, slot)

    for i in range(8):
        weigh(
            tasks(0, i, i + 1) + tasks(0, i, i + 1, segment=1) + tasks(1, i, i + 1)
        )
    swap_far()
    wait_sibling(1)
    wait_swap(1)
    for at in range(4):
        @pl.when(quarter == at)
        def _():
            for i in range(2):
                weigh(
                    tasks(2, 2 * i, 2 * i + 2, before=4 * (at % 2))
                    + tasks(3, i, i + 1, before=2 * at)
                )

    @pl.loop(0, SLOTS)
    def _(slot):
        take(2, slot)

    send_sibling(2)

    def home_copy(j):
        dst = out_hbm.at[:, pl.ds(pl.multiple_of(head * DH, DH), DH)]
        return packed.at[j], dst, SLOTS * half + j

    def home_remote(j):
        src, dst, target = home_copy(j)
        return pltpu.make_async_remote_copy(
            src_ref=src, dst_ref=dst, send_sem=out_send.at[j], recv_sem=out_recv.at[head],
            device_id=(outer, target), device_id_type=MESH,
        )

    def merge(j):
        for b in range(1, BRANCHES):
            r = 2**b
            count = ROWS // r
            rows = pl.ds(pl.multiple_of(QUERY_BASE[b] + j * count, count), count)
            out_b, lse_b = outs[rows, :], lse[rows, :]
            for at in range(r):
                rep_out[b - 1, pl.ds(at, count, stride=r), :] = out_b
                rep_lse[b - 1, pl.ds(at, count, stride=r), :] = lse_b

        row = lax.broadcasted_iota(jnp.int32, (ROWS, DH), 0)
        base = pl.ds(pl.multiple_of(j * ROWS, ROWS), ROWS)
        levels = [lse[base, :]]
        terms = [outs[base, :]]
        for b in range(1, BRANCHES):
            chosen = lax.bitwise_and(row, 2**b - 1) == offs[b]
            levels.append(jnp.where(chosen, rep_lse[b - 1], NEGATIVE))
            terms.append(rep_out[b - 1])
        top = functools.reduce(jnp.maximum, levels)
        weights = [jnp.exp2(level - top) for level in levels]
        above = sum(w * t for w, t in zip(weights, terms))
        packed[j] = (above / sum(weights)).astype(jnp.bfloat16)
        target = SLOTS * half + j

        @pl.when(target == inner)
        def _():
            src, dst, _ = home_copy(j)
            pltpu.make_async_copy(src, dst, out_recv.at[head]).start()

        @pl.when(target != inner)
        def _():
            home_remote(j).start()

    @pl.loop(0, 2)
    def _(step):
        side = lax.rem(step + x, 2)

        for which in range(2):
            @pl.when(side == which)
            def _():
                mix(tasks(0, 0, 8, segment=which) + tasks(1, 4 * which, 4 * which + 4))

        @pl.when(step == 0)
        def _():
            wait_sibling(2)
            wait_swap(2)

        for which in range(2):
            for at in range(4):
                @pl.when(jnp.logical_and(side == which, quarter == at))
                def _():
                    mix(
                        tasks(2, 2 * which, 2 * which + 2, before=4 * (at % 2))
                        + tasks(3, which, which + 1, before=2 * at)
                    )

        @pl.loop(0, 4)
        def _(at):
            up = lax.rem(at // 2 + y_hi + half, 2)
            merge(4 * side + 2 * up + lax.rem(at, 2))

    for a in range(3):
        @pl.when(jnp.logical_not(stays))
        def _():
            in_remote(a, 0).wait_send()

        for t in range(1, len(STEPS)):
            in_remote(a, t).wait_send()
    for a in (1, 2):
        @pl.when(y_lo == 0)
        def _():
            for h in range(HEADS):
                far_copy(a, h).wait_send()

        @pl.when(half == 0)
        def _():
            for kind in range(2):
                sibling_copy(a, kind).wait_send()

        @pl.when(y_lo == 1)
        def _():
            sibling_copy(a, 2).wait_send()
    for j in range(SLOTS):
        @pl.when(SLOTS * half + j != inner)
        def _():
            home_remote(j).wait_send()
    for h in range(HEADS):
        columns = out_hbm.at[:, h * DH : (h + 1) * DH]
        pltpu.make_async_copy(columns, columns, out_recv.at[h]).wait()


def local(queries, keys, values, offsets):
    anywhere = pl.BlockSpec(memory_space=pl.ANY)
    return pl.pallas_call(
        kernel,
        out_shape=jax.ShapeDtypeStruct((ROWS, HEADS * DH), jnp.bfloat16),
        in_specs=[pl.BlockSpec(memory_space=pltpu.SMEM), anywhere, anywhere, anywhere],
        out_specs=anywhere,
        scratch_shapes=[
            pltpu.VMEM((QUERY_ROWS, DH), jnp.bfloat16),
            pltpu.VMEM((KEY_ROWS, DH), jnp.bfloat16),
            pltpu.VMEM((KEY_ROWS, DH), jnp.bfloat16),
            pltpu.VMEM((ROWS, DH), jnp.float32),
            pltpu.VMEM((2, ROWS, HEADS * DH), jnp.bfloat16),
            pltpu.VMEM((2, HEADS * PICKED, DH), jnp.bfloat16),
            pltpu.VMEM((QUERY_ROWS, KEYS), jnp.bfloat16),
            pltpu.VMEM((3, TILE, KEYS), jnp.float32),
            pltpu.VMEM((QUERY_ROWS, DH), jnp.float32),
            pltpu.VMEM((QUERY_ROWS, DH), jnp.float32),
            pltpu.VMEM((BRANCHES - 1, ROWS, DH), jnp.float32),
            pltpu.VMEM((BRANCHES - 1, ROWS, DH), jnp.float32),
            pltpu.VMEM((SLOTS, ROWS, DH), jnp.bfloat16),
            pltpu.SemaphoreType.DMA((3, SLOTS)),
            pltpu.SemaphoreType.DMA((3, SLOTS)),
            pltpu.SemaphoreType.DMA((2,)),
            pltpu.SemaphoreType.DMA((2, HEADS)),
            pltpu.SemaphoreType.DMA((2, SLOTS)),
            pltpu.SemaphoreType.DMA((2, 3)),
            pltpu.SemaphoreType.DMA((2, 3)),
            pltpu.SemaphoreType.DMA((SLOTS,)),
            pltpu.SemaphoreType.DMA((HEADS,)),
        ],
        compiler_params=pltpu.CompilerParams(
            collective_id=0, has_side_effects=True, vmem_limit_bytes=60 * 2**20
        ),
        name="attention",
    )(offsets, queries, keys, values)


def solution(mesh):
    return jax.shard_map(
        local,
        mesh=mesh,
        in_specs=(
            P(("outer", "inner"), None),
            P(("outer", "inner"), None),
            P(("outer", "inner"), None),
            P(),
        ),
        out_specs=P(("outer", "inner"), None),
        check_vma=False,
    )
```

```python
import functools
import math

import jax
import jax.numpy as jnp
from jax import lax
from jax.experimental import pallas as pl
from jax.experimental.pallas import tpu as pltpu
from jax.sharding import PartitionSpec as P

KEYS = 2048
BRANCHES = 4
HEADS = 8
DH = 128
ROWS = 512
GROUP = 16
SLOTS = 8
SPAN = SLOTS * ROWS
PICKED = ROWS // 8
PAIRS = SLOTS // 2
TILE = 256
MESH = pl.DeviceIdType.MESH

QUERY_BASE = (0, 4096, 6144, 7168)
QUERY_ROWS = 7680
KEY_BASE = (0, 4096, 6144, 8192)
KEY_ROWS = 10240
LOG2E = math.log2(math.e)
TO_LOG2 = LOG2E * DH**-0.5
NEGATIVE = -1e30
STEPS = ((0, 0), (2, 1), (1, 0), (3, 1), (0, 1), (2, 0), (1, 1), (3, 0))


def kernel(
    off_ref, q_hbm, k_hbm, v_hbm, out_hbm,
    qa, ka, va, wide, home, far, probs, scores, lse, outs, rep_out, rep_lse, packed,
    in_send, in_recv, home_sem, far_send, far_recv, side_send, side_recv, out_send, out_recv,
):
    outer, inner = lax.axis_index("outer"), lax.axis_index("inner")
    head, half = inner // 2, inner % 2
    x, y_hi = inner // 4, (inner // 2) % 2
    own_slot, own_half = inner % SLOTS, inner // SLOTS
    y_lo = outer % 2
    quarter = 2 * y_lo + half
    offs = [off_ref[b, head] for b in range(BRANCHES)]

    barrier = pltpu.get_barrier_semaphore()
    for d in range(1, GROUP):
        pl.semaphore_signal(
            barrier, inc=1, device_id=(outer, lax.rem(inner + d, GROUP)), device_id_type=MESH
        )
    @pl.when(y_lo == 0)
    def _():
        for h in range(HEADS):
            pl.semaphore_signal(
                barrier, inc=1, device_id=(outer + 1, 2 * h + own_half), device_id_type=MESH
            )

    @pl.when(y_lo == 1)
    def _():
        for slot in range(SLOTS):
            pl.semaphore_signal(
                barrier, inc=1, device_id=(outer - 1, SLOTS * half + slot), device_id_type=MESH
            )

    @pl.when(y_lo == 0)
    def _():
        for a, source in ((0, k_hbm), (1, v_hbm)):
            load = pltpu.make_async_copy(source, home.at[a], home_sem.at[a])
            load.start()
        for a, source in ((0, k_hbm), (1, v_hbm)):
            pltpu.make_async_copy(source, home.at[a], home_sem.at[a]).wait()
            for h in range(HEADS):
                wide[...] = home[a, :, h * DH : (h + 1) * DH].astype(jnp.float32)
                picked = wide[pl.ds(off_ref[3, h], PICKED, stride=8), :]
                far[a, h * PICKED : (h + 1) * PICKED, :] = picked.astype(jnp.bfloat16)

    pl.semaphore_wait(barrier, GROUP - 1 + SLOTS)

    sources, buffers = (q_hbm, k_hbm, v_hbm), (qa, ka, va)

    def in_copy(a, t):
        dx, dy = STEPS[t]
        to_head = lax.rem(x + dx, 4) * 2 + lax.rem(y_hi + dy, 2)
        src = sources[a].at[:, pl.ds(pl.multiple_of(to_head * DH, DH), DH)]
        dst = buffers[a].at[pl.ds(pl.multiple_of(own_slot * ROWS, ROWS), ROWS)]
        return src, dst, 2 * to_head + own_half

    def in_remote(a, t):
        src, dst, target = in_copy(a, t)
        return pltpu.make_async_remote_copy(
            src_ref=src, dst_ref=dst, send_sem=in_send.at[a, t], recv_sem=in_recv.at[a, own_slot],
            device_id=(outer, target), device_id_type=MESH,
        )

    stays = half == own_half

    def send_in(a):
        @pl.when(stays)
        def _():
            src, dst, _ = in_copy(a, 0)
            pltpu.make_async_copy(src, dst, in_recv.at[a, own_slot]).start()

        @pl.when(jnp.logical_not(stays))
        def _():
            in_remote(a, 0).start()

        for t in range(1, len(STEPS)):
            in_remote(a, t).start()

    def far_copy(a, h):
        rows = buffers[a].at[
            pl.ds(pl.multiple_of(KEY_BASE[3] + own_half * ROWS + own_slot * PICKED, PICKED), PICKED)
        ]
        return pltpu.make_async_remote_copy(
            src_ref=far.at[a - 1, pl.ds(h * PICKED, PICKED)], dst_ref=rows,
            send_sem=far_send.at[a - 1, h], recv_sem=far_recv.at[a - 1, own_slot],
            device_id=(outer + 1, 2 * h + own_half), device_id_type=MESH,
        )

    def send_far(a):
        for h in range(HEADS):
            far_copy(a, h).start()

    send_in(1)
    send_in(0)

    @pl.when(y_lo == 0)
    def _():
        send_far(1)
        send_far(2)

    send_in(2)

    def take(a, slot):
        buffer = buffers[a]
        bases = QUERY_BASE if a == 0 else KEY_BASE
        shift = (0, 0, 0, 0) if a == 0 else (0, 0, half * (SPAN // 4), quarter * (SPAN // 8))
        rows = pl.ds(pl.multiple_of(slot * ROWS, ROWS), ROWS)
        arrived = buffer.at[rows]
        pltpu.make_async_copy(arrived, arrived, in_recv.at[a, slot]).wait()
        wide[...] = buffer[rows, :].astype(jnp.float32)
        for b in range(1, BRANCHES):
            count = ROWS >> b
            picked = wide[pl.ds(offs[b], count, stride=2**b), :]
            at = pl.multiple_of(bases[b] + shift[b] + slot * count, count)
            buffer[pl.ds(at, count), :] = picked.astype(jnp.bfloat16)

    def sibling_copy(a, kind):
        if kind == 0:
            rows = buffers[a].at[pl.ds(KEY_BASE[2], SPAN // 4)]
        elif kind == 1:
            rows = buffers[a].at[pl.ds(pl.multiple_of(KEY_BASE[3] + quarter * ROWS, ROWS), ROWS)]
        else:
            rows = buffers[a].at[pl.ds(pl.multiple_of(KEY_BASE[3] + half * ROWS, ROWS), ROWS)]
        return pltpu.make_async_remote_copy(
            src_ref=rows, dst_ref=rows,
            send_sem=side_send.at[a - 1, kind], recv_sem=side_recv.at[a - 1, kind],
            device_id=(outer, 2 * head + 1 - half), device_id_type=MESH,
        )

    def send_sibling(a):
        @pl.when(half == 0)
        def _():
            for kind in range(2):
                sibling_copy(a, kind).start()

    def swap_far():
        @pl.when(y_lo == 1)
        def _():
            for a in (1, 2):
                for slot in range(SLOTS):
                    rows = buffers[a].at[
                        pl.ds(pl.multiple_of(KEY_BASE[3] + half * ROWS + slot * PICKED, PICKED), PICKED)
                    ]
                    pltpu.make_async_copy(rows, rows, far_recv.at[a - 1, slot]).wait()
                sibling_copy(a, 2).start()

    def wait_rows(a, kind, first, count):
        rows = buffers[a].at[pl.ds(first, count)]
        pltpu.make_async_copy(rows, rows, side_recv.at[a - 1, kind]).wait()

    def wait_sibling(a):
        @pl.when(half == 1)
        def _():
            wait_rows(a, 0, KEY_BASE[2], SPAN // 4)
            wait_rows(a, 1, pl.multiple_of(KEY_BASE[3] + 2 * y_lo * ROWS, ROWS), ROWS)

    def wait_swap(a):
        @pl.when(y_lo == 1)
        def _():
            wait_rows(a, 2, pl.multiple_of(KEY_BASE[3] + (1 - half) * ROWS, ROWS), ROWS)

    allowed = lax.broadcasted_iota(jnp.int32, (TILE, TILE), 1) <= lax.broadcasted_iota(
        jnp.int32, (TILE, TILE), 0
    )

    def tasks(branch, first, last, before=0, segment=0):
        query = QUERY_BASE[branch] + segment * KEYS
        key = KEY_BASE[branch] + segment * KEYS
        return [(query + i * TILE, key, before + i + 1) for i in range(first, last)]

    def weigh(group):
        for n, (query, key, count) in enumerate(group):
            rows = slice(query, query + TILE)
            queries = qa[rows, :]
            tops = None
            for j in range(count):
                keys = ka[key + j * TILE : key + (j + 1) * TILE, :]
                s = lax.dot_general(
                    queries, keys, (((1,), (1,)), ((), ())), preferred_element_type=jnp.float32
                )
                if j == count - 1:
                    s = jnp.where(allowed, s, NEGATIVE)
                scores[n, :, j * TILE : (j + 1) * TILE] = s
                top = jnp.maximum(s[:, :128], s[:, 128:])
                tops = top if tops is None else jnp.maximum(tops, top)
            top = jnp.max(tops, axis=1, keepdims=True)
            sums = None
            for j in range(count):
                p = jnp.exp2((scores[n, :, j * TILE : (j + 1) * TILE] - top) * TO_LOG2)
                part = p[:, :128] + p[:, 128:]
                sums = part if sums is None else sums + part
                probs[rows, j * TILE : (j + 1) * TILE] = p.astype(jnp.bfloat16)
            total = jnp.sum(sums, axis=1, keepdims=True)
            lse[rows, :] = jnp.broadcast_to(top * TO_LOG2 + jnp.log(total) * LOG2E, (TILE, DH))
            outs[rows, :] = jnp.broadcast_to(1.0 / total, (TILE, DH))

    def mix(group):
        for query, key, count, size in group:
            rows = slice(query, query + size)
            weighted = jnp.dot(
                probs[rows, : count * TILE],
                va[key : key + count * TILE, :],
                preferred_element_type=jnp.float32,
            )
            outs[rows, :] = weighted * outs[rows, :]

    @pl.loop(0, SLOTS)
    def _(slot):
        take(1, slot)

    send_sibling(1)

    @pl.loop(0, SLOTS)
    def _(slot):
        take(0, slot)

    for i in range(8):
        weigh(
            tasks(0, i, i + 1) + tasks(0, i, i + 1, segment=1) + tasks(1, i, i + 1)
        )
    swap_far()
    wait_sibling(1)
    wait_swap(1)
    for at in range(4):
        @pl.when(quarter == at)
        def _():
            for i in range(2):
                weigh(
                    tasks(2, 2 * i, 2 * i + 2, before=4 * (at % 2))
                    + tasks(3, i, i + 1, before=2 * at)
                )

    @pl.loop(0, SLOTS)
    def _(slot):
        take(2, slot)

    send_sibling(2)

    def home_copy(j):
        dst = out_hbm.at[:, pl.ds(pl.multiple_of(head * DH, DH), DH)]
        return packed.at[j], dst, SLOTS * half + j

    def home_remote(j):
        src, dst, target = home_copy(j)
        return pltpu.make_async_remote_copy(
            src_ref=src, dst_ref=dst, send_sem=out_send.at[j], recv_sem=out_recv.at[head],
            device_id=(outer, target), device_id_type=MESH,
        )

    def merge(j):
        for b in range(1, BRANCHES):
            r = 2**b
            count = ROWS // r
            rows = pl.ds(pl.multiple_of(QUERY_BASE[b] + j * count, count), count)
            out_b, lse_b = outs[rows, :], lse[rows, :]
            for at in range(r):
                rep_out[b - 1, pl.ds(at, count, stride=r), :] = out_b
                rep_lse[b - 1, pl.ds(at, count, stride=r), :] = lse_b

        row = lax.broadcasted_iota(jnp.int32, (ROWS, DH), 0)
        base = pl.ds(pl.multiple_of(j * ROWS, ROWS), ROWS)
        levels = [lse[base, :]]
        terms = [outs[base, :]]
        for b in range(1, BRANCHES):
            chosen = lax.bitwise_and(row, 2**b - 1) == offs[b]
            levels.append(jnp.where(chosen, rep_lse[b - 1], NEGATIVE))
            terms.append(rep_out[b - 1])
        top = functools.reduce(jnp.maximum, levels)
        weights = [jnp.exp2(level - top) for level in levels]
        above = sum(w * t for w, t in zip(weights, terms))
        packed[j] = (above / sum(weights)).astype(jnp.bfloat16)
        target = SLOTS * half + j

        @pl.when(target == inner)
        def _():
            src, dst, _ = home_copy(j)
            pltpu.make_async_copy(src, dst, out_recv.at[head]).start()

        @pl.when(target != inner)
        def _():
            home_remote(j).start()

    def near(pair):
        group = tasks(0, 4 * (pair % 2), 4 * (pair % 2) + 4, segment=pair // 2)
        return [task + (TILE,) for task in group + tasks(1, 2 * pair, 2 * pair + 2)]

    def distant(pair, at):
        (task,) = tasks(2, pair, pair + 1, before=4 * (at % 2))
        last = (QUERY_BASE[3] + 128 * pair, KEY_BASE[3], 2 * at + pair // 2 + 1, 128)
        return [task + (TILE,), last]

    @pl.loop(0, PAIRS)
    def _(step):
        pair = lax.bitwise_xor(
            2 * lax.rem(x, 2) + jnp.where(stays, y_hi, 1 - y_hi), PAIRS - 1 - step
        )
        for which in range(PAIRS):
            @pl.when(pair == which)
            def _():
                mix(near(which))

        @pl.when(step == 0)
        def _():
            wait_sibling(2)
            wait_swap(2)

        for which in range(PAIRS):
            for at in range(4):
                @pl.when(jnp.logical_and(pair == which, quarter == at))
                def _():
                    mix(distant(which, at))

        for core in range(2):
            merge(2 * pair + core)

    for a in range(3):
        @pl.when(jnp.logical_not(stays))
        def _():
            in_remote(a, 0).wait_send()

        for t in range(1, len(STEPS)):
            in_remote(a, t).wait_send()
    for a in (1, 2):
        @pl.when(y_lo == 0)
        def _():
            for h in range(HEADS):
                far_copy(a, h).wait_send()

        @pl.when(half == 0)
        def _():
            for kind in range(2):
                sibling_copy(a, kind).wait_send()

        @pl.when(y_lo == 1)
        def _():
            sibling_copy(a, 2).wait_send()
    for j in range(SLOTS):
        @pl.when(SLOTS * half + j != inner)
        def _():
            home_remote(j).wait_send()
    for h in range(HEADS):
        columns = out_hbm.at[:, h * DH : (h + 1) * DH]
        pltpu.make_async_copy(columns, columns, out_recv.at[h]).wait()


def local(queries, keys, values, offsets):
    anywhere = pl.BlockSpec(memory_space=pl.ANY)
    return pl.pallas_call(
        kernel,
        out_shape=jax.ShapeDtypeStruct((ROWS, HEADS * DH), jnp.bfloat16),
        in_specs=[pl.BlockSpec(memory_space=pltpu.SMEM), anywhere, anywhere, anywhere],
        out_specs=anywhere,
        scratch_shapes=[
            pltpu.VMEM((QUERY_ROWS, DH), jnp.bfloat16),
            pltpu.VMEM((KEY_ROWS, DH), jnp.bfloat16),
            pltpu.VMEM((KEY_ROWS, DH), jnp.bfloat16),
            pltpu.VMEM((ROWS, DH), jnp.float32),
            pltpu.VMEM((2, ROWS, HEADS * DH), jnp.bfloat16),
            pltpu.VMEM((2, HEADS * PICKED, DH), jnp.bfloat16),
            pltpu.VMEM((QUERY_ROWS, KEYS), jnp.bfloat16),
            pltpu.VMEM((3, TILE, KEYS), jnp.float32),
            pltpu.VMEM((QUERY_ROWS, DH), jnp.float32),
            pltpu.VMEM((QUERY_ROWS, DH), jnp.float32),
            pltpu.VMEM((BRANCHES - 1, ROWS, DH), jnp.float32),
            pltpu.VMEM((BRANCHES - 1, ROWS, DH), jnp.float32),
            pltpu.VMEM((SLOTS, ROWS, DH), jnp.bfloat16),
            pltpu.SemaphoreType.DMA((3, SLOTS)),
            pltpu.SemaphoreType.DMA((3, SLOTS)),
            pltpu.SemaphoreType.DMA((2,)),
            pltpu.SemaphoreType.DMA((2, HEADS)),
            pltpu.SemaphoreType.DMA((2, SLOTS)),
            pltpu.SemaphoreType.DMA((2, 3)),
            pltpu.SemaphoreType.DMA((2, 3)),
            pltpu.SemaphoreType.DMA((SLOTS,)),
            pltpu.SemaphoreType.DMA((HEADS,)),
        ],
        compiler_params=pltpu.CompilerParams(
            collective_id=0, has_side_effects=True, vmem_limit_bytes=60 * 2**20
        ),
        name="attention",
    )(offsets, queries, keys, values)


def solution(mesh):
    return jax.shard_map(
        local,
        mesh=mesh,
        in_specs=(
            P(("outer", "inner"), None),
            P(("outer", "inner"), None),
            P(("outer", "inner"), None),
            P(),
        ),
        out_specs=P(("outer", "inner"), None),
        check_vma=False,
    )
```
